32 devices in a mesh: row: 8 (over z, x), col: 4 (over y, core).
Axes of the slice: x: 2, y: 2, z: 4, core: 2. Of those that a mesh axis runs over, the one named last changes fastest.
Arguments:
- pair: bfloat16 [1536, 1536, 128], P('row', 'col'), may hold values from -6 to 6
- gain_in: float32 [128], replicated, may hold values from 0.25 to 1.75
- w_a_gate: bfloat16 [128, 128], replicated, may hold values from -0.5 to 0.5
- w_a: bfloat16 [128, 128], replicated, may hold values from -0.5 to 0.5
- w_b_gate: bfloat16 [128, 128], replicated, may hold values from -0.5 to 0.5
- w_b: bfloat16 [128, 128], replicated, may hold values from -0.5 to 0.5
- w_out_gate: bfloat16 [128, 128], replicated, may hold values from -0.5 to 0.5
- w_out: bfloat16 [128, 128], replicated, may hold values from -0.5 to 0.5
- gain_out: float32 [128], replicated, may hold values from 0.25 to 1.75
Outputs:
- update: bfloat16 [1536, 1536, 128], P('row', 'col')
The draws below stay inside these ranges and needn't reach their ends.
All inputs are finite; a program needn't handle non-finite values.
Results may differ from the reference program's by a relative error of at most 0.0083.
Values may be sent and summed in bfloat16 or wider, within the bound.
A program may use at most 256 MiB of HBM per device.

```python
import jax
import jax.numpy as jnp
from jax import lax

C = 128
N = 1536


def block_scale(own_key, shape, shards, smallest, top_value):
    loudness, own = 1.0, jax.random.fold_in(own_key, 6)
    for dim, blocks in shards:
        draws = jnp.exp(jax.random.uniform(jax.random.fold_in(own, dim), (blocks,), jnp.float32, smallest / len(shards), top_value / len(shards)))
        loudness = loudness * jnp.repeat(draws, shape[dim] // blocks).reshape([-1 if axis == dim else 1 for axis in range(len(shape))])
    return loudness


def bell_draw(own_key, extent, scale, limit, shards=(), held_as=jnp.bfloat16):
    loudness = block_scale(own_key, extent, shards, -0.22, 0.18) if shards else 1.0
    array = jax.random.normal(own_key, extent, jnp.float32) * scale * loudness
    return jnp.minimum(jnp.maximum(array, -limit), limit).astype(held_as)


def setup_inputs(seed: int = 0) -> dict:
    key_of = jax.random.split(jax.random.key(seed), 10)
    return {
        "pair": bell_draw(key_of[0], (N, N, C), 1.0, 6.0, ((0, 8), (1, 4))),
        "gain_in": jnp.clip(1.0 + 0.15 * jax.random.normal(key_of[1], (C,), jnp.float32), 0.25, 1.75),
        "w_a_gate": bell_draw(key_of[2], (C, C), C ** -0.5, 0.5),
        "w_a": bell_draw(key_of[3], (C, C), C ** -0.5, 0.5),
        "w_b_gate": bell_draw(key_of[4], (C, C), C ** -0.5, 0.5),
        "w_b": bell_draw(key_of[5], (C, C), C ** -0.5, 0.5),
        "w_out_gate": bell_draw(key_of[6], (C, C), C ** -0.5, 0.5),
        "w_out": bell_draw(key_of[7], (C, C), C ** -0.5, 0.5),
        "gain_out": jnp.clip(1.0 + 0.15 * jax.random.normal(key_of[8], (C,), jnp.float32), 0.25, 1.75),
    }


def layer_norm_last(values, gain):
    centred = values - lax.optimization_barrier(jnp.mean(values, axis=-1, keepdims=True))
    variance = lax.optimization_barrier(jnp.mean(centred * centred, axis=-1, keepdims=True))
    return centred * lax.rsqrt(variance + 1e-05) * gain

def project(normed, weight):
    return jnp.einsum('ijd,de->ije', normed.astype(jnp.float32), weight.astype(jnp.float32))

def reference(pair, gain_in, w_a_gate, w_a, w_b_gate, w_b, w_out_gate, w_out, gain_out):
    blocks = 16
    height = N // blocks

    def front(zblock):
        normed = layer_norm_last(zblock.astype(jnp.float32), gain_in).astype(jnp.bfloat16)
        left = (jax.nn.sigmoid(project(normed, w_a_gate)) * project(normed, w_a)).astype(jnp.bfloat16)
        right = (jax.nn.sigmoid(project(normed, w_b_gate)) * project(normed, w_b)).astype(jnp.bfloat16)
        return (left, right)
    left, right = lax.map(front, pair.reshape(blocks, height, N, C))
    left = left.reshape(N, N, C).transpose(2, 0, 1)
    right = right.reshape(N, N, C).transpose(2, 0, 1)

    def contract(operands):
        lhs, rhs = operands
        return jnp.einsum('cki,ckj->cij', lhs.astype(jnp.float32), rhs.astype(jnp.float32)).astype(jnp.bfloat16)
    summed = lax.map(contract, (left.reshape(C // 8, 8, N, N), right.reshape(C // 8, 8, N, N)))
    summed = summed.reshape(C, N, N)
    summed_blocks = summed.reshape(C, blocks, height, N).transpose(1, 0, 2, 3)

    def finish(operands):
        oblock, zblock = operands
        normed = layer_norm_last(zblock.astype(jnp.float32), gain_in).astype(jnp.bfloat16)
        gating = jax.nn.sigmoid(project(normed, w_out_gate))
        values = oblock.astype(jnp.float32)
        centred = values - lax.optimization_barrier(jnp.mean(values, axis=0, keepdims=True))
        variance = lax.optimization_barrier(jnp.mean(centred * centred, axis=0, keepdims=True))
        scaled = (centred * lax.rsqrt(variance + 1e-05) * gain_out[:, None, None]).astype(jnp.bfloat16)
        projected = jnp.einsum('cij,cd->ijd', scaled.astype(jnp.float32), w_out.astype(jnp.float32))
        return (gating * projected).astype(jnp.bfloat16)
    update = lax.map(finish, (summed_blocks, pair.reshape(blocks, height, N, C)))
    return update.reshape(N, N, C)
```

```python
import functools

import jax
import jax.numpy as jnp
from jax import lax
from jax.experimental import pallas as pl
from jax.experimental.pallas import tpu as pltpu
from jax.sharding import Mesh, PartitionSpec as P

BF16, F32 = jnp.bfloat16, jnp.float32
ROWS = 16
GROUP = ("rlo", "col")
VMEM_LIMIT = 56 * 1024 * 1024


def norm_last(x, gain):
    values = x.astype(F32)
    centred = values - jnp.mean(values, axis=-1, keepdims=True)
    variance = jnp.mean(centred * centred, axis=-1, keepdims=True)
    return (centred * lax.rsqrt(variance + 1e-05) * gain).astype(BF16)


def dot(a, b, da, db):
    return lax.dot_general(a, b, (((da,), (db,)), ((), ())), preferred_element_type=F32)


def gated(both):
    c = both.shape[0] // 2
    return jax.nn.sigmoid(both[:c]) * both[c:]


def front_kernel(S, M, w, x_ref, gain_ref, wl_ref, wr_ref, l0_ref, l1_ref, r0_ref, r1_ref, lscr, rscr):
    c = lscr.shape[0]
    half = c // 2

    def step(k, carry):
        xn = norm_last(x_ref[k], gain_ref[...])
        rscr[:, k, :] = gated(dot(wr_ref[...], xn, 1, 1))
        parts = [
            xn[(s * M + m) * w : (s * M + m + 1) * w] for m in range(M) for s in range(S)
        ]
        lscr[:, k, :] = gated(dot(wl_ref[...], jnp.concatenate(parts, axis=0), 1, 1))
        return carry

    lax.fori_loop(0, x_ref.shape[0], step, 0)
    width = S * w
    for q, (l_ref, r_ref) in enumerate(((l0_ref, r0_ref), (l1_ref, r1_ref))):
        r_ref[...] = rscr[q * half : (q + 1) * half].astype(BF16)
        for m in range(M):
            l_ref[m] = lscr[q * half : (q + 1) * half, :, m * width : (m + 1) * width].astype(BF16)


def front(pair, gain, wl, wr, S, M, w):
    K, J, C = pair.shape
    half, width = C // 2, S * w
    fixed = lambda i: (0, 0)
    lspec = pl.BlockSpec((M, half, ROWS, width), lambda i: (0, 0, i, 0))
    rspec = pl.BlockSpec((half, ROWS, J), lambda i: (0, i, 0))
    lshape = jax.ShapeDtypeStruct((M, half, K, width), BF16)
    rshape = jax.ShapeDtypeStruct((half, K, J), BF16)
    return pl.pallas_call(
        functools.partial(front_kernel, S, M, w),
        grid=(K // ROWS,),
        in_specs=[
            pl.BlockSpec((ROWS, J, C), lambda i: (i, 0, 0)),
            pl.BlockSpec((1, C), fixed),
            pl.BlockSpec((2 * C, C), fixed),
            pl.BlockSpec((2 * C, C), fixed),
        ],
        out_specs=[lspec, lspec, rspec, rspec],
        out_shape=[lshape, lshape, rshape, rshape],
        scratch_shapes=[pltpu.VMEM((C, ROWS, J), F32), pltpu.VMEM((C, ROWS, J), F32)],
        compiler_params=pltpu.CompilerParams(vmem_limit_bytes=VMEM_LIMIT),
        cost_estimate=pl.CostEstimate(
            flops=8 * K * J * C * C, bytes_accessed=6 * K * J * C, transcendentals=2 * K * J * C
        ),
    )(pair, gain.reshape(1, C), wl, wr)


def contract_kernel(S, w, add, which_ref, l_ref, r_ref, *rest):
    got_ref, out_ref = (rest[0], rest[-1]) if add else (None, rest[-1])
    rlo, cols, _, k, width = l_ref.shape
    ncol, J = r_ref.shape[1], r_ref.shape[4]
    lhs = jnp.concatenate(
        [l_ref[:, ci, 0].reshape(rlo * k, width) for ci in range(cols)], axis=1
    )
    lhs = lhs.T
    for cj in range(ncol):
        acc = dot(lhs, r_ref[:, cj, 0].reshape(rlo * k, J), 1, 0)
        acc = acc.reshape(cols * S, w, J)
        if add:
            acc = acc + got_ref[:, cj, 0].astype(F32)
        out_ref[:, cj, 0] = acc.astype(BF16)


def contract(which, l, r, S, w, got=None, after=None):
    rlo, ncol, g, k, width = l.shape
    J = r.shape[4]
    cols = ncol // 2
    pspec = pl.BlockSpec((cols * S, ncol, 1, w, J), lambda i, h: (0, 0, i, 0, 0))
    in_specs = [
        pl.BlockSpec((rlo, cols, 1, k, width), lambda i, h: (0, h[0], i, 0, 0)),
        pl.BlockSpec((rlo, ncol, 1, k, J), lambda i, h: (0, 0, i, 0, 0)),
    ]
    operands = [l, r]
    if got is not None:
        in_specs.append(pspec)
        operands.append(got)
    if after is not None:
        in_specs.append(pl.BlockSpec(memory_space=pl.ANY))
        operands.append(after)
    size = g * cols * width * ncol * J
    return pl.pallas_call(
        functools.partial(contract_kernel, S, w, got is not None),
        grid_spec=pltpu.PrefetchScalarGridSpec(
            num_scalar_prefetch=1, grid=(g,), in_specs=in_specs, out_specs=pspec
        ),
        out_shape=jax.ShapeDtypeStruct((cols * S, ncol, g, w, J), BF16),
        compiler_params=pltpu.CompilerParams(vmem_limit_bytes=VMEM_LIMIT),
        cost_estimate=pl.CostEstimate(
            flops=2 * size * rlo * k,
            bytes_accessed=2 * (size + r.size + l.size // 2),
            transcendentals=0,
        ),
    )(which, *operands)


def finish_kernel(v0_ref, v1_ref, x_ref, gin_ref, gout_ref, wg_ref, wo_ref, *rest):
    out_ref, scr = rest[-2], rest[-1]
    half = scr.shape[0] // 2
    scr[:half] = v0_ref[...].astype(F32)
    scr[half:] = v1_ref[...].astype(F32)

    def step(i, carry):
        values = scr[:, i, :]
        centred = values - jnp.mean(values, axis=0, keepdims=True)
        variance = jnp.mean(centred * centred, axis=0, keepdims=True)
        scaled = (centred * lax.rsqrt(variance + 1e-05) * gout_ref[...]).astype(BF16)
        projected = dot(scaled, wo_ref[...], 0, 0)
        gate = jax.nn.sigmoid(dot(norm_last(x_ref[i], gin_ref[...]), wg_ref[...], 1, 0))
        out_ref[i] = (gate * projected).astype(BF16)
        return carry

    lax.fori_loop(0, x_ref.shape[0], step, 0)


def finish(v0, v1, pair, gain_in, gain_out, wg, wo, base, before):
    K, J, C = pair.shape
    half, w, _ = v0.shape
    fixed = lambda i: (0, 0)
    vspec = pl.BlockSpec((half, ROWS, J), lambda i: (0, i, 0))
    xspec = pl.BlockSpec((ROWS, J, C), lambda i: (base // ROWS + i, 0, 0))
    in_specs = [
        vspec,
        vspec,
        xspec,
        pl.BlockSpec((1, C), fixed),
        pl.BlockSpec((C, 1), fixed),
        pl.BlockSpec((C, C), fixed),
        pl.BlockSpec((C, C), fixed),
    ]
    operands = [v0, v1, pair, gain_in.reshape(1, C), gain_out.reshape(C, 1), wg, wo]
    aliases = {}
    if before is not None:
        in_specs.append(pl.BlockSpec(memory_space=pl.ANY))
        aliases = {len(operands): 0}
        operands.append(before)
    return pl.pallas_call(
        finish_kernel,
        grid=(w // ROWS,),
        in_specs=in_specs,
        out_specs=xspec,
        out_shape=jax.ShapeDtypeStruct((K, J, C), BF16),
        scratch_shapes=[pltpu.VMEM((C, ROWS, J), F32)],
        input_output_aliases=aliases,
        compiler_params=pltpu.CompilerParams(vmem_limit_bytes=VMEM_LIMIT),
        cost_estimate=pl.CostEstimate(
            flops=4 * w * J * C * C, bytes_accessed=6 * w * J * C, transcendentals=w * J * C
        ),
    )(*operands)


def local(rlo, ncol, pair, gain_in, w_a_gate, w_a, w_b_gate, w_b, w_out_gate, w_out, gain_out):
    K, J, C = pair.shape
    D = rlo * ncol
    S = J // K
    w = 128 // S
    M = K // w
    half = C // 2
    g = half // D
    h = lax.axis_index("half").astype(jnp.int32)
    mine, other = h.reshape(1), (1 - h).reshape(1)
    swap = [(0, 1), (1, 0)]

    wl = jnp.concatenate([w_a_gate.T, w_a.T], axis=0)
    wr = jnp.concatenate([w_b_gate.T, w_b.T], axis=0)
    l0, l1, r0, r1 = front(pair, gain_in, wl, wr, S, M, w)
    lefts, rights = (l0, l1), (r0, r1)

    def spread(block):
        got = lax.all_to_all(block.reshape(D, g, K, -1), GROUP, 0, 0)
        return got.reshape(rlo, ncol, g, K, -1)

    def tie(value, after):
        return value if after is None else lax.optimization_barrier((value, after))[0]

    items = [(q, m) for q in range(2) for m in range(M)]
    held_r, held_l, came, back = {}, {}, {}, {}
    out = None

    def prepare(t, after):
        q, m = items[t]
        if q not in held_r:
            held_r[q] = spread(tie(rights[q], after))
        held_l[t] = spread(tie(lefts[q][m], after))
        sent = contract(other, held_l[t], held_r[q], S, w)
        came[t] = lax.ppermute(sent, "half", swap)
        return sent

    def consume(t, after):
        nonlocal out
        q, m = items[t]
        total = contract(mine, held_l.pop(t), held_r[q], S, w, came.pop(t), after)
        ret = lax.all_to_all(total.reshape(D, g, w, J), GROUP, 0, 0)
        back[t] = ret.reshape(half, w, J)
        if q == 1:
            out = finish(
                back.pop(m), back.pop(t), pair, gain_in, gain_out, w_out_gate, w_out, m * w, out
            )
        return total

    last = prepare(0, None)
    last = prepare(1, last)
    held_r[1] = spread(tie(rights[1], last))
    for t in range(len(items)):
        done = consume(t, last)
        if t + 2 < len(items):
            last = prepare(t + 2, done)
        else:
            last = None
    return out


def solution(mesh):
    rows, ncol = mesh.shape["row"], mesh.shape["col"]
    split = Mesh(mesh.devices.reshape(2, rows // 2, ncol), ("half", "rlo", "col"))
    spec = P(("half", "rlo"), "col", None)
    in_specs = (spec, P(), P(), P(), P(), P(), P(), P(), P())
    return jax.shard_map(
        functools.partial(local, rows // 2, ncol),
        mesh=split,
        in_specs=in_specs,
        out_specs=spec,
        check_vma=False,
    )
```

```python
import functools

import jax
import jax.numpy as jnp
from jax import lax
from jax.experimental import pallas as pl
from jax.experimental.pallas import tpu as pltpu
from jax.sharding import Mesh, PartitionSpec as P

BF16, F32 = jnp.bfloat16, jnp.float32
ROWS = 16
GROUP = ("rlo", "col")
VMEM_LIMIT = 56 * 1024 * 1024


def norm_last(x, gain):
    values = x.astype(F32)
    centred = values - jnp.mean(values, axis=-1, keepdims=True)
    variance = jnp.mean(centred * centred, axis=-1, keepdims=True)
    return (centred * lax.rsqrt(variance + 1e-05) * gain).astype(BF16)


def dot(a, b, da, db):
    return lax.dot_general(a, b, (((da,), (db,)), ((), ())), preferred_element_type=F32)


def gated(both):
    c = both.shape[0] // 2
    return jax.nn.sigmoid(both[:c]) * both[c:]


def transfers(kinds, srcs, dsts, send, recv, own):
    h, rlo, col = (lax.axis_index(name) for name in ("half", "rlo", "col"))
    nlo, ncol = lax.axis_size("rlo"), lax.axis_size("col")
    D = nlo * ncol
    me = rlo * ncol + col
    mesh_id = pl.DeviceIdType.MESH
    across = (1 - h, rlo, col)
    has_swap = "swap" in kinds
    has_spread = "spread" in kinds

    def peer(step):
        return lax.rem(me + step, D)

    def place(p):
        return (h, p // ncol, lax.rem(p, ncol))

    def spread(n, step):
        return pltpu.make_async_remote_copy(
            src_ref=srcs[n].at[peer(step)],
            dst_ref=dsts[n].at[me],
            send_sem=send.at[n, step],
            recv_sem=recv.at[n, step],
            device_id=place(peer(step)),
            device_id_type=mesh_id,
        )

    def swap(n):
        return pltpu.make_async_remote_copy(
            src_ref=srcs[n],
            dst_ref=dsts[n],
            send_sem=send.at[n, 0],
            recv_sem=recv.at[n, 0],
            device_id=across,
            device_id_type=mesh_id,
        )

    def keep(n):
        return pltpu.make_async_copy(srcs[n].at[me], dsts[n].at[me], own.at[n])

    def begin():
        barrier = pltpu.get_barrier_semaphore()
        count = 0
        if has_swap:
            pl.semaphore_signal(barrier, inc=1, device_id=across, device_id_type=mesh_id)
            count += 1
        if has_spread:
            def greet(step, carry):
                pl.semaphore_signal(
                    barrier, inc=1, device_id=place(peer(step)), device_id_type=mesh_id
                )
                return carry

            lax.fori_loop(1, D, greet, 0)
            count += D - 1
        pl.semaphore_wait(barrier, count)
        for n, kind in enumerate(kinds):
            if kind == "swap":
                swap(n).start()
        for n, kind in enumerate(kinds):
            if kind == "spread":
                keep(n).start()

                def go(step, carry):
                    spread(n, step).start()
                    return carry

                lax.fori_loop(1, D, go, 0)

    def end():
        for n, kind in enumerate(kinds):
            if kind == "spread":
                keep(n).wait()

                def settle(step, carry):
                    spread(n, step).wait()
                    return carry

                lax.fori_loop(1, D, settle, 0)
        for n, kind in enumerate(kinds):
            if kind == "swap":
                swap(n).wait()

    return begin, end


def call(kernel, grid, in_specs, out_specs, out_shapes, scratch, operands, comm, cid, aliases=None):
    kinds = [kind for kind, _ in comm]
    srcs = [src for _, src in comm]
    n, n_in, n_out, n_scr = len(comm), len(operands), len(out_shapes), len(scratch)
    anywhere = pl.BlockSpec(memory_space=pl.ANY)
    aliases = aliases or {}
    D = lax.axis_size("rlo") * lax.axis_size("col")
    sems = []
    if n:
        sems = [
            pltpu.SemaphoreType.DMA((n, D)),
            pltpu.SemaphoreType.DMA((n, D)),
            pltpu.SemaphoreType.DMA((n,)),
        ]

    def body(*refs):
        ins, rest = refs[:n_in], refs[n_in:]
        src_refs, rest = rest[:n], rest[n:]
        outs, rest = rest[:n_out], rest[n_out:]
        dst_refs, rest = rest[:n], rest[n:]
        scr, sem = rest[:n_scr], rest[n_scr:]
        if n:
            begin, end = transfers(kinds, src_refs, dst_refs, *sem)
            pl.when(pl.program_id(0) == 0)(begin)
        if kernel is not None:
            kernel(*ins, *outs, *scr)
        if n:
            pl.when(pl.program_id(0) == grid[0] - 1)(end)

    params = dict(vmem_limit_bytes=VMEM_LIMIT)
    if n:
        params.update(collective_id=cid, has_side_effects=True)
    return pl.pallas_call(
        body,
        grid=grid,
        in_specs=[*in_specs, *[anywhere] * n],
        out_specs=[*out_specs, *[anywhere] * n],
        out_shape=[*out_shapes, *[jax.ShapeDtypeStruct(x.shape, x.dtype) for x in srcs]],
        scratch_shapes=[*scratch, *sems],
        input_output_aliases=aliases,
        compiler_params=pltpu.CompilerParams(**params),
    )(*operands, *srcs)


def front_kernel(S, M, w, x_ref, gain_ref, wl_ref, wr_ref, l_ref, r_ref, lscr, rscr):
    def step(k, carry):
        xn = norm_last(x_ref[k], gain_ref[...])
        rscr[:, k, :] = gated(dot(wr_ref[...], xn, 1, 1))
        parts = [
            xn[(s * M + m) * w : (s * M + m + 1) * w] for m in range(M) for s in range(S)
        ]
        lscr[:, k, :] = gated(dot(wl_ref[...], jnp.concatenate(parts, axis=0), 1, 1))
        return carry

    lax.fori_loop(0, x_ref.shape[0], step, 0)
    width = S * w
    r_ref[...] = rscr[...].astype(BF16)
    for m in range(M):
        l_ref[m] = lscr[:, :, m * width : (m + 1) * width].astype(BF16)


def front(pair, gain, wl, wr, S, M, w, comm=(), cid=None):
    K, J, C = pair.shape
    half, width = C // 2, S * w
    fixed = lambda i: (0, 0)
    return call(
        functools.partial(front_kernel, S, M, w),
        (K // ROWS,),
        [
            pl.BlockSpec((ROWS, J, C), lambda i: (i, 0, 0)),
            pl.BlockSpec((1, C), fixed),
            pl.BlockSpec((C, C), fixed),
            pl.BlockSpec((C, C), fixed),
        ],
        [
            pl.BlockSpec((M, half, ROWS, width), lambda i: (0, 0, i, 0)),
            pl.BlockSpec((half, ROWS, J), lambda i: (0, i, 0)),
        ],
        [
            jax.ShapeDtypeStruct((M, half, K, width), BF16),
            jax.ShapeDtypeStruct((half, K, J), BF16),
        ],
        [pltpu.VMEM((half, ROWS, J), F32), pltpu.VMEM((half, ROWS, J), F32)],
        [pair, gain.reshape(1, C), wl, wr],
        comm,
        cid,
    )


def contract_kernel(S, w, add, which_ref, l_ref, r_ref, *rest):
    got_ref, out_ref = (rest[0], rest[-1]) if add else (None, rest[-1])
    rlo, cols, _, k, width = l_ref.shape
    ncol, J = r_ref.shape[1], r_ref.shape[4]
    lhs = jnp.concatenate(
        [l_ref[:, ci, 0].reshape(rlo * k, width) for ci in range(cols)], axis=1
    )
    lhs = lhs.T
    for cj in range(ncol):
        acc = dot(lhs, r_ref[:, cj, 0].reshape(rlo * k, J), 1, 0)
        acc = acc.reshape(cols * S, w, J)
        if add:
            acc = acc + got_ref[:, cj, 0].astype(F32)
        out_ref[:, cj, 0] = acc.astype(BF16)


def contract(which, l, r, S, w, got=None, after=None):
    rlo, ncol, g, k, width = l.shape
    J = r.shape[4]
    cols = ncol // 2
    pspec = pl.BlockSpec((cols * S, ncol, 1, w, J), lambda i, h: (0, 0, i, 0, 0))
    in_specs = [
        pl.BlockSpec((rlo, cols, 1, k, width), lambda i, h: (0, h[0], i, 0, 0)),
        pl.BlockSpec((rlo, ncol, 1, k, J), lambda i, h: (0, 0, i, 0, 0)),
    ]
    operands = [l, r]
    if got is not None:
        in_specs.append(pspec)
        operands.append(got)
    if after is not None:
        in_specs.append(pl.BlockSpec(memory_space=pl.ANY))
        operands.append(after)
    size = g * cols * width * ncol * J
    return pl.pallas_call(
        functools.partial(contract_kernel, S, w, got is not None),
        grid_spec=pltpu.PrefetchScalarGridSpec(
            num_scalar_prefetch=1, grid=(g,), in_specs=in_specs, out_specs=pspec
        ),
        out_shape=jax.ShapeDtypeStruct((cols * S, ncol, g, w, J), BF16),
        compiler_params=pltpu.CompilerParams(vmem_limit_bytes=VMEM_LIMIT),
        cost_estimate=pl.CostEstimate(
            flops=2 * size * rlo * k,
            bytes_accessed=2 * (size + r.size + l.size // 2),
            transcendentals=0,
        ),
    )(which, *operands)


def finish_kernel(v0_ref, v1_ref, x_ref, gin_ref, gout_ref, wg_ref, wo_ref, *rest):
    out_ref, scr = rest[-2], rest[-1]
    half = scr.shape[0] // 2
    scr[:half] = v0_ref[...].astype(F32)
    scr[half:] = v1_ref[...].astype(F32)

    def step(i, carry):
        values = scr[:, i, :]
        centred = values - jnp.mean(values, axis=0, keepdims=True)
        variance = jnp.mean(centred * centred, axis=0, keepdims=True)
        scaled = (centred * lax.rsqrt(variance + 1e-05) * gout_ref[...]).astype(BF16)
        projected = dot(scaled, wo_ref[...], 0, 0)
        gate = jax.nn.sigmoid(dot(norm_last(x_ref[i], gin_ref[...]), wg_ref[...], 1, 0))
        out_ref[i] = (gate * projected).astype(BF16)
        return carry

    lax.fori_loop(0, x_ref.shape[0], step, 0)


def finish(v0, v1, pair, gain_in, gain_out, wg, wo, base, before, comm=(), cid=None):
    K, J, C = pair.shape
    half, w, _ = v0.shape
    fixed = lambda i: (0, 0)
    vspec = pl.BlockSpec((half, ROWS, J), lambda i: (0, i, 0))
    xspec = pl.BlockSpec((ROWS, J, C), lambda i: (base // ROWS + i, 0, 0))
    in_specs = [
        vspec,
        vspec,
        xspec,
        pl.BlockSpec((1, C), fixed),
        pl.BlockSpec((C, 1), fixed),
        pl.BlockSpec((C, C), fixed),
        pl.BlockSpec((C, C), fixed),
    ]
    operands = [v0, v1, pair, gain_in.reshape(1, C), gain_out.reshape(C, 1), wg, wo]
    aliases = {}
    if before is not None:
        in_specs.append(pl.BlockSpec(memory_space=pl.ANY))
        aliases = {len(operands): 0}
        operands.append(before)
    return call(
        finish_kernel,
        (w // ROWS,),
        in_specs,
        [xspec],
        [jax.ShapeDtypeStruct((K, J, C), BF16)],
        [pltpu.VMEM((C, ROWS, J), F32)],
        operands,
        comm,
        cid,
        aliases,
    )


def local(rlo, ncol, pair, gain_in, w_a_gate, w_a, w_b_gate, w_b, w_out_gate, w_out, gain_out):
    K, J, C = pair.shape
    D = rlo * ncol
    S = J // K
    w = 128 // S
    M = K // w
    half = C // 2
    g = half // D
    h = lax.axis_index("half").astype(jnp.int32)
    mine, other = h.reshape(1), (1 - h).reshape(1)

    def weights(gate, value, q):
        part = slice(q * half, (q + 1) * half)
        return jnp.concatenate([gate[:, part].T, value[:, part].T], axis=0)

    def project(q, comm=(), cid=None):
        wl, wr = weights(w_a_gate, w_a, q), weights(w_b_gate, w_b, q)
        return front(pair, gain_in, wl, wr, S, M, w, comm, cid)

    def grouped(block):
        return block.reshape(D, g, -1, block.shape[-1])

    def received(block):
        return block.reshape(rlo, ncol, g, K, -1)

    def closing(m, out, comm=(), cid=None):
        v0, v1 = back[m].reshape(half, w, J), back[M + m].reshape(half, w, J)
        return finish(
            v0, v1, pair, gain_in, gain_out, w_out_gate, w_out, m * w, out, comm, cid
        )

    items = [(q, m) for q in range(2) for m in range(M)]
    T = len(items)
    lefts, rights, held_r, held_l, back = {}, {}, {}, {}, {}
    lefts[0], rights[0] = project(0)
    comm = [("spread", grouped(rights[0])), ("spread", grouped(lefts[0][0]))]
    lefts[1], rights[1], got_r, got_l = project(1, comm, 0)
    held_r[0], held_l[0] = received(got_r), received(got_l)
    parts = [grouped(rights[1])[:, i * g // M : (i + 1) * g // M] for i in range(M)]
    parts = [part for part in parts if part.shape[1]]
    got_parts = []
    out, total = None, None
    for t in range(T):
        q, m = items[t]
        comm = [("swap", contract(other, held_l[t], held_r[q], S, w))]
        names = ["swap"]
        if total is not None:
            comm.append(("spread", total.reshape(D, g, w, J)))
            names.append("back")
        if t + 1 < T:
            nq, nm = items[t + 1]
            comm.append(("spread", grouped(lefts[nq][nm])))
            names.append("left")
        if t < len(parts):
            comm.append(("spread", parts[t]))
            names.append("right")
        if t >= M + 2:
            out, *got = closing(t - M - 2, out, comm, t + 1)
        else:
            got = call(None, (1,), [], [], [], [], [], comm, t + 1)
        got = dict(zip(names, got))
        if "back" in got:
            back[t - 1] = got["back"]
        if "left" in got:
            held_l[t + 1] = received(got["left"])
        if "right" in got:
            got_parts.append(got["right"])
            if len(got_parts) == len(parts):
                held_r[1] = received(jnp.concatenate(got_parts, axis=1))
        total = contract(mine, held_l.pop(t), held_r[q], S, w, got["swap"])
    out, back[T - 1] = closing(M - 2, out, [("spread", total.reshape(D, g, w, J))], T + 1)
    (out,) = closing(M - 1, out)
    return out


def solution(mesh):
    rows, ncol = mesh.shape["row"], mesh.shape["col"]
    split = Mesh(mesh.devices.reshape(2, rows // 2, ncol), ("half", "rlo", "col"))
    spec = P(("half", "rlo"), "col", None)
    in_specs = (spec, P(), P(), P(), P(), P(), P(), P(), P())
    return jax.shard_map(
        functools.partial(local, rows // 2, ncol),
        mesh=split,
        in_specs=in_specs,
        out_specs=spec,
        check_vma=False,
    )
```
